256 devices in a mesh: mat: 2 (over y_lo), band: 8 (over x, core), col: 16 (over z, y_hi).
Axes of the slice: x: 4, y: 4 (y_hi: 2, y_lo: 2; y = y_hi * 2 + y_lo), z: 8, core: 2. Of those that a mesh axis runs over, the one named last changes fastest.
Arguments:
- iterate: float32 [8192, 18432], P(('mat', 'band'), 'col'), parts along dimension 0, may hold values from -6 to 6
Outputs:
- next_iterate: float32 [8192, 18432], P(('mat', 'band'), 'col'), parts along dimension 0
The draws below stay inside these ranges and needn't reach their ends.
There are 2 independent parts, one for each index of `mat`. The reference program is written for one: setup_inputs(seed, part) draws one part's arguments, and reference() takes and returns one part's arrays. A program takes and returns all parts, laid end to end along the dimension named above; each array names one. Nothing has to cross between parts.
All inputs are finite; a program needn't handle non-finite values.
Results may differ from the reference program's by a relative error of at most 0.012.
The reference program's roundings to bfloat16 on the way (of `narrow`, `gram_half` and `poly`) count: a program that leaves them out, or rounds other values in their place, can miss the bound.
Values may be sent and summed in bfloat16 or wider, within the bound.
A program may use at most 128 MiB of HBM per device.

```python
import jax
import jax.numpy as jnp

ROWS = 4096
COLS = 18432


def block_scale(key, shape, split, smallest, top_value):
    gain, own = 1.0, jax.random.fold_in(key, 6)
    for axis_at, blocks in split:
        draws = jnp.exp(jax.random.uniform(jax.random.fold_in(own, axis_at), (blocks,), jnp.float32, smallest / len(split), top_value / len(split)))
        gain = gain * jnp.repeat(draws, shape[axis_at] // blocks).reshape([-1 if axis == axis_at else 1 for axis in range(len(shape))])
    return gain


def gaussian(rng, extent, spread, most, pieces=(), kind=jnp.bfloat16):
    loudness = block_scale(rng, extent, pieces, -0.22, 0.18) if pieces else 1.0
    result = jax.random.normal(rng, extent, jnp.float32) * spread * loudness
    return jnp.minimum(jnp.maximum(result, -most), most).astype(kind)


def setup_inputs(seed: int = 0, part: int = 0) -> dict:
    streams_of = jax.random.split(jax.random.key(seed), 2)
    part_splits = jax.random.split(jax.random.fold_in(streams_of[1], part), 2)
    return {
        "iterate": gaussian(part_splits[0], (ROWS, COLS), 1.0, 6.0, ((0, 8), (1, 16)), jnp.float32),
    }


linear_coef = 3.4445
cubic_coef = -4.7750
quintic_coef = 2.0315


def reference(iterate):
    narrow = iterate.astype(jnp.bfloat16)
    gram = jnp.dot(narrow, narrow.T, preferred_element_type=jnp.float32) / COLS
    gram_half = gram.astype(jnp.bfloat16)
    square = jnp.dot(gram_half, gram_half, preferred_element_type=jnp.float32)
    poly = (cubic_coef * gram + quintic_coef * square).astype(jnp.bfloat16)
    return linear_coef * iterate + jnp.dot(poly, narrow, preferred_element_type=jnp.float32)
```

```python
import jax
import jax.numpy as jnp
from jax import lax
from jax.experimental import pallas as pl
from jax.experimental.pallas import tpu as pltpu
from jax.sharding import PartitionSpec as P

COLS = 18432
MESH = pl.DeviceIdType.MESH
linear_coef = 3.4445
cubic_coef = -4.775
quintic_coef = 2.0315

F32, BF16 = jnp.float32, jnp.bfloat16
BLOCK, WIDTH, TICKS, UNIT = 512, 1152, 8, 64
ROWS = BLOCK * TICKS
SPLIT = 1536
MESSAGES = 400
START = (0, 1, 3, 5, 7, 9, 10, 11)


def dot(a, b, contract):
    return lax.dot_general(a, b, (((1,), (contract,)), ((), ())), preferred_element_type=F32)


def kernel(x_ref, o_ref, X, N, Y, V, G, SB0, RB0, SB, RB, YS, YR, FS, FR, GS, DS, DR, DB, YA, ssem, rsem, lsem):
    mat, band, col = lax.axis_index("mat"), lax.axis_index("band"), lax.axis_index("col")
    x, core = lax.div(band, 2), lax.rem(band, 2)
    z, y = lax.div(col, 2), lax.rem(col, 2)
    other = 1 - y

    def at_x(d):
        return (mat, lax.rem(x + d + 4, 4) * 2 + core, col)

    def zi(d):
        return lax.rem(z + d + 8, 8)

    def at_z(d):
        return (mat, band, zi(d) * 2 + y)

    XP, XM, ZP, ZM = at_x(1), at_x(-1), at_z(1), at_z(-1)
    YP = (mat, band, z * 2 + other)
    CP = (mat, x * 2 + 1 - core, col)

    started = []

    def send(src, dst, peer):
        n = len(started)
        copy = pltpu.make_async_remote_copy(
            src_ref=src, dst_ref=dst, send_sem=ssem.at[n], recv_sem=rsem.at[n], device_id=peer, device_id_type=MESH
        )
        copy.start()
        started.append(copy)
        return copy

    loads = [pltpu.make_async_copy(x_ref.at[pl.ds(UNIT * u, UNIT)], X.at[u], lsem.at[u]) for u in range(8)]
    for load in loads:
        load.start()
    barrier = pltpu.get_barrier_semaphore()
    for peer in (XP, XM, ZP, ZM, YP, CP):
        pl.semaphore_signal(barrier, inc=1, device_id=peer, device_id_type=MESH)
    for u, load in enumerate(loads):
        load.wait()
        N[0, u] = X[u].astype(BF16)
    pl.semaphore_wait(barrier, 6)

    plus, minus, pair, hop, hop_pair = {}, {}, {}, {}, {}
    relay = {}

    def send_own(i):
        plus[i] = send(N.at[0, pl.ds(2 * i, 2)], N.at[2 + i, pl.ds(0, 2)], XP)
        minus[i] = send(N.at[0, pl.ds(2 * i, 2)], N.at[2 + i, pl.ds(4, 2)], XM)

    def send_hop(i):
        if i < 2:
            hop[i] = send(N.at[2 + i, pl.ds(0, 2)], N.at[6, pl.ds(2 * i, 2)], XP)
        else:
            hop[i] = send(N.at[2 + i, pl.ds(4, 2)], N.at[6, pl.ds(2 * i, 2)], XM)

    def pass_hop(i):
        hop[i].wait_recv()
        hop_pair[i] = send(N.at[6, pl.ds(2 * i, 2)], N.at[7, pl.ds(2 * i, 2)], CP)

    send_own(0)
    pair_block = send(N.at[0], N.at[1], CP)
    send_own(1)

    def arrive(t):
        if t == 1:
            pair_block.wait_recv()
        if 2 <= t <= 5:
            i = t - 2
            plus[i].wait_recv()
            relay[i, 0] = send(N.at[t, pl.ds(0, 2)], N.at[t, pl.ds(2, 2)], CP)
            minus[i].wait_recv()
            relay[i, 1] = send(N.at[t, pl.ds(4, 2)], N.at[t, pl.ds(6, 2)], CP)
            if i < 2:
                send_own(i + 2)
            else:
                send_hop(i - 2)
                send_hop(i)
            relay[i, 0].wait_recv()
            relay[i, 1].wait_recv()

    first, step0, step, last, moved = {}, {}, {}, {}, {}
    diag = {}

    def gram(t):
        arrive(t)
        if t <= 5:
            right = N[t].reshape(BLOCK, WIDTH)
        elif t == 6:
            right = N[2:6, 4:6].reshape(BLOCK, WIDTH)
        else:
            right = N[2:6, 2:4].reshape(BLOCK, WIDTH)
        total = jnp.zeros((1, BLOCK), F32)
        for m in range(2):
            if t <= 5:
                left = N[0, 4 * m : 4 * m + 4].reshape(256, WIDTH)
            elif t == 6:
                left = N[2 + 2 * m : 4 + 2 * m, 0:2].reshape(256, WIDTH)
            else:
                left = N[2 + 2 * m : 4 + 2 * m, 4:6].reshape(256, WIDTH)
            p = dot(left, right, 1)
            if t == 0:
                rows = lax.broadcasted_iota(jnp.int32, (256, BLOCK), 0) + 256 * m
                lanes = lax.broadcasted_iota(jnp.int32, (256, BLOCK), 1)
                total += jnp.sum(jnp.where(rows == lanes, p, 0.0), axis=0, keepdims=True)
            p = p.reshape(4, UNIT, BLOCK)
            low, high = p[:, 0:32, 256:], p[:, 32:64, 256:]
            V[t, 4 * m : 4 * m + 4, 0:64, :] = p[:, :, 0:256]
            V[t, 4 * m : 4 * m + 4, 64:96, :] = jnp.where(y == 0, low, high)
            YS[t, 4 * m : 4 * m + 4] = jnp.where(y == 0, high, low).astype(BF16)
        first[t] = send(YS.at[t], YR.at[t], YP)
        if t == 0:
            DS[...] = jnp.broadcast_to(total, (8, BLOCK))
            diag["y"] = send(DS, DR, YP)

    def stage1(t):
        first[t].wait_recv()
        V[t, :, 64:96, :] += YR[t].astype(F32)
        d = zi(4)
        SB0[t, 0] = V[t, d, :, 0:128].astype(BF16)
        SB0[t, 1] = V[t, d, :, 128:256].astype(BF16)
        step0[t] = (send(SB0.at[t, 0], RB0.at[t, 0], ZP), send(SB0.at[t, 1], RB0.at[t, 1], ZM))

    def stage2(t):
        step0[t][0].wait_recv()
        d = zi(3)
        SB[t, 0, 0, :, 0:128] = (V[t, d, :, 0:128] + RB0[t, 0].astype(F32)).astype(BF16)
        SB[t, 0, 0, :, 128:256] = V[t, d, :, 128:256].astype(BF16)
        up = send(SB.at[t, 0, 0], RB.at[t, 0, 0], ZP)
        step0[t][1].wait_recv()
        d = zi(-3)
        SB[t, 1, 0, :, 0:128] = V[t, d, :, 0:128].astype(BF16)
        SB[t, 1, 0, :, 128:256] = (V[t, d, :, 128:256] + RB0[t, 1].astype(F32)).astype(BF16)
        step[t, 0] = (up, send(SB.at[t, 1, 0], RB.at[t, 1, 0], ZM))

    def stage34(t, n):
        both = []
        for way, peer in ((0, ZP), (1, ZM)):
            step[t, n - 1][way].wait_recv()
            d = zi(3 - n) if way == 0 else zi(n - 3)
            SB[t, way, n] = (V[t, d] + RB[t, way, n - 1].astype(F32)).astype(BF16)
            both.append(send(SB.at[t, way, n], RB.at[t, way, n], peer))
        step[t, n] = both

    def stage5(t):
        step[t, 2][0].wait_recv()
        step[t, 2][1].wait_recv()
        r = V[t, z] + RB[t, 0, 2].astype(F32) + RB[t, 1, 2].astype(F32)
        V[t, z] = r
        FS[t] = jnp.where(y == 0, r[32:64], r[0:32]).astype(BF16)
        last[t] = send(FS.at[t], FR.at[t], YP)

    def stage6(t):
        last[t].wait_recv()
        r = V[t, z]
        mine = jnp.where(y == 0, r[0:32], r[32:64]) + FR[t].astype(F32)
        g = jnp.concatenate([mine, r[64:96]], axis=1) * (1.0 / COLS)
        if t == 0:
            rows = lax.broadcasted_iota(jnp.int32, (32, BLOCK), 0) + (z * 64 + y * 32)
            lanes = lax.broadcasted_iota(jnp.int32, (32, BLOCK), 1)
            g = jnp.where(rows == lanes, DS[0:1], g)
        g = g.astype(BF16)
        if t <= 5:
            G[z, y, :, BLOCK * t : BLOCK * (t + 1)] = g
        else:
            GS[t - 6] = g
            there = G.at[z, y, :, pl.ds(BLOCK * t, BLOCK)]
            moved[t] = send(GS.at[t - 6], there, XM if t == 6 else XP)

    def diag_step(r):
        if r == 1:
            diag["y"].wait_recv()
            DB[z] = DS[...] + DR[...]
            diag[1] = (send(DB.at[z], DB.at[z], ZP), send(DB.at[z], DB.at[z], ZM))
        elif r <= 4:
            diag[r - 1][0].wait_recv()
            back = zi(1 - r)
            up = send(DB.at[back], DB.at[back], ZP)
            diag[r - 1][1].wait_recv()
            ahead = zi(r - 1)
            diag[r] = (up, send(DB.at[ahead], DB.at[ahead], ZM) if r < 4 else None)
        elif r == 5:
            diag[4][0].wait_recv()
            diag["y"].wait_send()
            DS[...] = jnp.sum(DB[...], axis=0) * (1.0 / COLS)

    stages = {0: gram, 1: stage1, 2: stage2, 3: lambda t: stage34(t, 1), 4: lambda t: stage34(t, 2), 5: stage5, 6: stage6}
    for r in range(START[-1] + 7):
        if 1 <= r <= 5:
            diag_step(r)
        for t in range(TICKS):
            if 1 <= r - START[t] <= 6:
                stages[r - START[t]](t)
        for t in range(TICKS):
            if r == START[t]:
                gram(t)
        if r == 14:
            pass_hop(0)
            pass_hop(2)
    moved[6].wait_recv()
    moved[7].wait_recv()

    sent_y, served, hops, hops_pair = {}, {}, {}, {}

    def unit(q):
        u = zi(q)
        return u, lax.div(u, 2), lax.rem(u, 2)

    def products(qs):
        n = len(qs)

        def body(t, _):
            lanes = pl.ds(pl.multiple_of(t * BLOCK, BLOCK), BLOCK)
            left = jnp.concatenate([G[zi(q), :, :, lanes].reshape(UNIT, BLOCK) for q in qs], axis=0)
            p = dot(left, N[t].reshape(BLOCK, WIDTH), 0)

            @pl.when(t == 0)
            def _():
                YA[0 : UNIT * n] = p

            @pl.when(t > 0)
            def _():
                YA[0 : UNIT * n] += p

            return 0

        lax.fori_loop(0, TICKS, body, 0)
        for i, q in enumerate(qs):
            u, half, odd = unit(q)
            Y[0, u] = YA[UNIT * i : UNIT * (i + 1)].astype(BF16)
            sent_y[q] = (
                send(Y.at[0, u], Y.at[2 + half, odd], XP),
                send(Y.at[0, u], Y.at[2 + half, 4 + odd], XM),
                send(Y.at[0, u], Y.at[1, u], CP),
            )
        for i, q in enumerate(qs):
            u = zi(q)
            rows = G[u].reshape(UNIT, ROWS).astype(F32)
            square = jnp.sum(rows * rows, axis=1, keepdims=True)
            here = lax.broadcasted_iota(jnp.int32, (UNIT, BLOCK), 0) + u * UNIT
            lanes = lax.broadcasted_iota(jnp.int32, (UNIT, BLOCK), 1)
            g = jnp.sum(jnp.where(here == lanes, DS[0:1], 0.0), axis=1, keepdims=True)
            half = g.astype(BF16).astype(F32)
            poly = (cubic_coef * g + quintic_coef * square).astype(BF16).astype(F32)
            fix = poly - (cubic_coef * half + quintic_coef * square)
            X[u] = linear_coef * X[u] + cubic_coef * YA[UNIT * i : UNIT * (i + 1)] + fix * N[0, u].astype(F32)

    def serve(qs):
        for q in qs:
            u, half, odd = unit(q)
            sent_y[q][0].wait_recv()
            if q in (0, 1, 2, 3):
                hops[q] = send(Y.at[2 + half, odd], Y.at[6, u], XP)
            a = send(Y.at[2 + half, odd], Y.at[2 + half, 2 + odd], CP)
            sent_y[q][1].wait_recv()
            if q not in (0, 1, 2, 3):
                hops[q] = send(Y.at[2 + half, 4 + odd], Y.at[6, u], XM)
            b = send(Y.at[2 + half, 4 + odd], Y.at[2 + half, 6 + odd], CP)
            served[q] = (a, b)

    def pass_y(qs):
        for q in qs:
            hops[q].wait_recv()
            u = zi(q)
            hops_pair[q] = send(Y.at[6, u], Y.at[7, u], CP)

    wide, thin = pl.ds(SPLIT, ROWS - SPLIT), pl.ds(0, SPLIT)
    to_y = {}
    to_y["thin"] = send(G.at[z, y, :, thin], G.at[z, y, :, thin], YP)
    own = [(send(G.at[z, y], G.at[z, y], ZP), send(G.at[z, y], G.at[z, y], ZM))]
    to_y[0] = [send(G.at[z, y, :, wide], G.at[z, y, :, wide], YP)]
    to_y["thin"].wait_recv()
    theirs = [
        (
            send(G.at[z, other, :, thin], G.at[z, other, :, thin], ZP),
            send(G.at[z, other, :, thin], G.at[z, other, :, thin], ZM),
        )
    ]
    pass_hop(1)
    pass_hop(3)
    to_y[0][0].wait_recv()
    for i in range(4):
        hop_pair[i].wait_recv()
    products([0])

    done = [[0]]
    for k in range(1, 5):
        qs = [-k, k] if k < 4 else [4]
        forward, to_y[k] = [], []
        for way, q, peer in ((0, -k, ZP), (1, k, ZM)):
            own[k - 1][way].wait_recv()
            u = zi(q)
            if k < 3:
                forward.append(send(G.at[u, y], G.at[u, y], peer))
            elif k == 3:
                part = pl.ds(ROWS // 2 * way, ROWS // 2)
                forward.append(send(G.at[u, y, :, part], G.at[u, y, :, part], peer))
            if k < 4:
                to_y[k].append(send(G.at[u, y, :, wide], G.at[u, y, :, wide], YP))
        if k == 4:
            u = zi(4)
            to_y[k].append(send(G.at[u, y, :, wide], G.at[u, y, :, wide], YP))
        own.append(forward)
        forward = []
        for way, q, peer in ((0, -k, ZP), (1, k, ZM)):
            theirs[k - 1][way].wait_recv()
            u = zi(q)
            if k < 3:
                forward.append(send(G.at[u, other, :, thin], G.at[u, other, :, thin], peer))
            elif k == 3:
                part = pl.ds(SPLIT // 2 * way, SPLIT // 2)
                forward.append(send(G.at[u, other, :, part], G.at[u, other, :, part], peer))
        theirs.append(forward)
        for copy in to_y[k]:
            copy.wait_recv()
        products(qs)
        serve(done[-1])
        if k >= 2:
            pass_y(done[-2])
        done.append(qs)

    def add_up(t, m):
        left = G[4 * m : 4 * m + 4, :, :, BLOCK * t : BLOCK * (t + 1)].reshape(256, BLOCK)
        p = dot(left, Y[t].reshape(BLOCK, WIDTH), 0)
        X[4 * m : 4 * m + 4] += quintic_coef * p.reshape(4, UNIT, WIDTH)

    for q in sent_y:
        sent_y[q][2].wait_recv()
    for t in (0, 1):
        for m in range(2):
            add_up(t, m)
    serve([4])
    pass_y([-3, 3])
    for q in served:
        served[q][0].wait_recv()
        served[q][1].wait_recv()
    for t in (2, 3, 4, 5):
        for m in range(2):
            add_up(t, m)
    pass_y([4])
    for m in range(2):
        add_up(6, m)
    for q in hops_pair:
        hops_pair[q].wait_recv()
    stores = []
    for m in range(2):
        add_up(7, m)
        for u in range(4 * m, 4 * m + 4):
            stores.append(pltpu.make_async_copy(X.at[u], o_ref.at[pl.ds(UNIT * u, UNIT)], lsem.at[u]))
            stores[-1].start()
    for copy in started:
        if copy is not diag["y"]:
            copy.wait_send()
    for store in stores:
        store.wait()


def shards(iterate):
    scratch = [
        pltpu.VMEM((8, UNIT, WIDTH), F32),
        pltpu.VMEM((TICKS, 8, UNIT, WIDTH), BF16),
        pltpu.VMEM((TICKS, 8, UNIT, WIDTH), BF16),
        pltpu.VMEM((TICKS, 8, 96, 256), F32),
        pltpu.VMEM((8, 2, 32, ROWS), BF16),
        pltpu.VMEM((TICKS, 2, 96, 128), BF16),
        pltpu.VMEM((TICKS, 2, 96, 128), BF16),
        pltpu.VMEM((TICKS, 2, 3, 96, 256), BF16),
        pltpu.VMEM((TICKS, 2, 3, 96, 256), BF16),
        pltpu.VMEM((TICKS, 8, 32, 256), BF16),
        pltpu.VMEM((TICKS, 8, 32, 256), BF16),
        pltpu.VMEM((TICKS, 32, 256), BF16),
        pltpu.VMEM((TICKS, 32, 256), BF16),
        pltpu.VMEM((2, 32, BLOCK), BF16),
        pltpu.VMEM((8, BLOCK), F32),
        pltpu.VMEM((8, BLOCK), F32),
        pltpu.VMEM((8, 8, BLOCK), F32),
        pltpu.VMEM((2 * UNIT, WIDTH), F32),
        pltpu.SemaphoreType.DMA((MESSAGES,)),
        pltpu.SemaphoreType.DMA((MESSAGES,)),
        pltpu.SemaphoreType.DMA((8,)),
    ]
    return pl.pallas_call(
        kernel,
        out_shape=jax.ShapeDtypeStruct(iterate.shape, F32),
        in_specs=[pl.BlockSpec(memory_space=pl.ANY)],
        out_specs=pl.BlockSpec(memory_space=pl.ANY),
        scratch_shapes=scratch,
        compiler_params=pltpu.CompilerParams(
            collective_id=0, has_side_effects=True, vmem_limit_bytes=60 * 1024 * 1024
        ),
        cost_estimate=pl.CostEstimate(flops=6 * BLOCK * ROWS * WIDTH, bytes_accessed=8 * BLOCK * WIDTH, transcendentals=0),
    )(iterate)


def solution(mesh):
    return jax.shard_map(
        shards,
        mesh=mesh,
        in_specs=(P(("mat", "band"), "col"),),
        out_specs=P(("mat", "band"), "col"),
        check_vma=False,
    )
```

```python
import jax
import jax.numpy as jnp
from jax import lax
from jax.experimental import pallas as pl
from jax.experimental.pallas import tpu as pltpu
from jax.sharding import PartitionSpec as P

COLS = 18432
MESH = pl.DeviceIdType.MESH
linear_coef = 3.4445
cubic_coef = -4.775
quintic_coef = 2.0315

F32, BF16 = jnp.float32, jnp.bfloat16
BLOCK, WIDTH, TICKS, UNIT = 512, 1152, 8, 64
ROWS = BLOCK * TICKS
SPLIT = 1536
MESSAGES, SENDS = 216, 48
START = (0, 1, 2, 4, 5, 7, 7, 7)
FLIGHT = 4


def dot(a, b, contract):
    return lax.dot_general(a, b, (((1,), (contract,)), ((), ())), preferred_element_type=F32)


def kernel(x_ref, o_ref, X, N, Y, V, G, SA, RA, SH, RH, SB, RB, SC, RC, RD, YS, YR, FS, FR, GS, DS, DR, DB, YA, ssem, rsem, lsem):
    mat, band, col = lax.axis_index("mat"), lax.axis_index("band"), lax.axis_index("col")
    x, core = lax.div(band, 2), lax.rem(band, 2)
    z, y = lax.div(col, 2), lax.rem(col, 2)
    other = 1 - y

    def at_x(d):
        return (mat, lax.rem(x + d + 4, 4) * 2 + core, col)

    def zi(d):
        return lax.rem(z + d + 8, 8)

    def at_z(d):
        return (mat, band, zi(d) * 2 + y)

    XP, XM, ZP, ZM, ZPP, ZMM = at_x(1), at_x(-1), at_z(1), at_z(-1), at_z(2), at_z(-2)
    YP = (mat, band, z * 2 + other)
    ZPY, ZMY = (mat, band, zi(1) * 2 + other), (mat, band, zi(-1) * 2 + other)
    CP = (mat, x * 2 + 1 - core, col)

    started = []

    def send(src, dst, peer):
        n = len(started)
        if n >= SENDS:
            started[n - SENDS].wait_send()
        copy = pltpu.make_async_remote_copy(
            src_ref=src,
            dst_ref=dst,
            send_sem=ssem.at[n % SENDS],
            recv_sem=rsem.at[n],
            device_id=peer,
            device_id_type=MESH,
        )
        copy.start()
        started.append(copy)
        return copy

    loads = [pltpu.make_async_copy(x_ref.at[pl.ds(UNIT * u, UNIT)], X.at[u], lsem.at[u]) for u in range(8)]
    for load in loads:
        load.start()
    barrier = pltpu.get_barrier_semaphore()
    for peer in (XP, XM, ZP, ZM, ZPP, ZMM, ZPY, ZMY, YP, CP):
        pl.semaphore_signal(barrier, inc=1, device_id=peer, device_id_type=MESH)
    for u, load in enumerate(loads):
        load.wait()
        N[0, u] = X[u].astype(BF16)
    pl.semaphore_wait(barrier, 10)

    plus, minus, pair, hop, hop_pair = {}, {}, {}, {}, {}
    relay = {}

    def send_own(i):
        plus[i] = send(N.at[0, pl.ds(2 * i, 2)], N.at[2 + i, pl.ds(0, 2)], XP)
        minus[i] = send(N.at[0, pl.ds(2 * i, 2)], N.at[2 + i, pl.ds(4, 2)], XM)

    def send_hop(i):
        if i < 2:
            hop[i] = send(N.at[2 + i, pl.ds(0, 2)], N.at[6, pl.ds(2 * i, 2)], XP)
        else:
            hop[i] = send(N.at[2 + i, pl.ds(4, 2)], N.at[6, pl.ds(2 * i, 2)], XM)

    def pass_hop(i):
        hop[i].wait_recv()
        hop_pair[i] = send(N.at[6, pl.ds(2 * i, 2)], N.at[7, pl.ds(2 * i, 2)], CP)

    send_own(0)
    pair_block = send(N.at[0], N.at[1], CP)
    for i in range(1, FLIGHT):
        send_own(i)

    def arrive(t):
        if t == 1:
            pair_block.wait_recv()
        if 2 <= t <= 5:
            i = t - 2
            plus[i].wait_recv()
            relay[i, 0] = send(N.at[t, pl.ds(0, 2)], N.at[t, pl.ds(2, 2)], CP)
            minus[i].wait_recv()
            relay[i, 1] = send(N.at[t, pl.ds(4, 2)], N.at[t, pl.ds(6, 2)], CP)
            if i + FLIGHT < 4:
                send_own(i + FLIGHT)
            if i >= 2:
                send_hop(i - 2)
                send_hop(i)
            relay[i, 0].wait_recv()
            relay[i, 1].wait_recv()

    first, own_part, ring1, ring2, ring3, moved, diag = {}, {}, {}, {}, {}, {}, {}

    def height(t):
        return 96 if t < 6 else 128

    def gram(t):
        arrive(t)
        if t <= 5:
            right = N[t].reshape(BLOCK, WIDTH)
        elif t == 6:
            right = N[2:6, 4:6].reshape(BLOCK, WIDTH)
        else:
            right = N[2:6, 2:4].reshape(BLOCK, WIDTH)
        total = jnp.zeros((1, BLOCK), F32)
        for m in range(2):
            if t <= 5:
                left = N[0, 4 * m : 4 * m + 4].reshape(256, WIDTH)
            elif t == 6:
                left = N[2 + 2 * m : 4 + 2 * m, 0:2].reshape(256, WIDTH)
            else:
                left = N[2 + 2 * m : 4 + 2 * m, 4:6].reshape(256, WIDTH)
            p = dot(left, right, 1)
            if t == 0:
                rows = lax.broadcasted_iota(jnp.int32, (256, BLOCK), 0) + 256 * m
                lanes = lax.broadcasted_iota(jnp.int32, (256, BLOCK), 1)
                total += jnp.sum(jnp.where(rows == lanes, p, 0.0), axis=0, keepdims=True)
            p = p.reshape(4, UNIT, BLOCK)
            low, high = p[:, 0:32], p[:, 32:64]
            mine, rest = jnp.where(y == 0, low, high), jnp.where(y == 0, high, low)
            here = pl.ds(4 * m, 4)
            V[t, here, 0:32, :] = mine[:, :, 0:256]
            V[t, here, 32:64, :] = mine[:, :, 256:]
            V[t, here, 64:96, :] = rest[:, :, 0:256]
            if t < 6:
                YS[t, here] = rest[:, :, 256:].astype(BF16)
            else:
                V[t, here, 96:128, :] = rest[:, :, 256:]
        if t < 6:
            first[t] = send(YS.at[t], YR.at[t], YP)
        else:
            launch(t)
        if t == 0:
            DS[...] = jnp.broadcast_to(total, (8, BLOCK))
            diag["y"] = send(DS, DR, YP)

    def stage1(t):
        if t < 6:
            first[t].wait_recv()
            V[t, :, 32:64, :] += YR[t].astype(F32)
            launch(t)

    def launch(t):
        h = height(t)
        sent = []
        for way, peer, far in ((0, ZP, ZPP), (1, ZM, ZMM)):
            d = zi(3) if way == 0 else zi(-3)
            SA[t, way, 0:h] = V[t, d, 0:h].astype(BF16)
            sent.append(send(SA.at[t, way, pl.ds(0, h)], RA.at[t, way, pl.ds(0, h)], peer))
            SH[t, way, 0:h] = V[t, zi(4), 0:h, 128 * way : 128 * way + 128].astype(BF16)
            sent.append(send(SH.at[t, way, pl.ds(0, h)], RH.at[t, way, pl.ds(0, h)], far))
        ring1[t] = sent
        FS[t, 0 : h - 64] = V[t, z, 64:h].astype(BF16)
        own_part[t] = send(FS.at[t, pl.ds(0, h - 64)], FR.at[t, pl.ds(0, h - 64)], YP)

    def stage2(t):
        h = height(t)
        sent = []
        for way, peer in ((0, ZP), (1, ZM)):
            ring1[t][2 * way].wait_recv()
            ring1[t][2 * way + 1].wait_recv()
            d = zi(2) if way == 0 else zi(-2)
            half, rest = pl.ds(128 * way, 128), pl.ds(128 - 128 * way, 128)
            SB[t, way, 0:h, half] = (
                V[t, d, 0:h, half] + RA[t, way, 0:h, half].astype(F32) + RH[t, way, 0:h].astype(F32)
            ).astype(BF16)
            SB[t, way, 0:h, rest] = (V[t, d, 0:h, rest] + RA[t, way, 0:h, rest].astype(F32)).astype(BF16)
            sent.append(send(SB.at[t, way, pl.ds(0, h)], RB.at[t, way, pl.ds(0, h)], peer))
        ring2[t] = sent

    def stage3(t):
        h = height(t)
        sent = []
        for way, peer, across in ((0, ZP, ZPY), (1, ZM, ZMY)):
            ring2[t][way].wait_recv()
            d = zi(1) if way == 0 else zi(-1)
            SC[t, way, 0:h] = (V[t, d, 0:h] + RB[t, way, 0:h].astype(F32)).astype(BF16)
            sent.append(send(SC.at[t, way, pl.ds(0, 64)], RC.at[t, way], peer))
            sent.append(send(SC.at[t, way, pl.ds(64, h - 64)], RD.at[t, way, pl.ds(0, h - 64)], across))
        ring3[t] = sent

    def stage4(t):
        for copy in ring3[t]:
            copy.wait_recv()
        own_part[t].wait_recv()
        r = V[t, z, 0:64] + RC[t, 0].astype(F32) + RC[t, 1].astype(F32)
        n = height(t) - 64
        cross = RD[t, 0, 0:n].astype(F32) + RD[t, 1, 0:n].astype(F32) + FR[t, 0:n].astype(F32)
        low, high = r[0:32] + cross[0:32], r[32:64]
        if n == 64:
            high = high + cross[32:64]
        g = (jnp.concatenate([low, high], axis=1) * (1.0 / COLS)).astype(BF16)
        if t < 6:
            G[z, y, :, BLOCK * t : BLOCK * (t + 1)] = g
        else:
            GS[t - 6] = g
            there = G.at[z, y, :, pl.ds(BLOCK * t, BLOCK)]
            moved[t] = send(GS.at[t - 6], there, XM if t == 6 else XP)

    def stage5(t):
        if t >= 6:
            moved[t].wait_recv()

    def diag_step(r):
        if r == 1:
            diag["y"].wait_recv()
            DB[z] = DS[...] + DR[...]
            diag[1] = (send(DB.at[z], DB.at[z], ZP), send(DB.at[z], DB.at[z], ZM))
        elif r <= 4:
            diag[r - 1][0].wait_recv()
            back = zi(1 - r)
            up = send(DB.at[back], DB.at[back], ZP)
            diag[r - 1][1].wait_recv()
            ahead = zi(r - 1)
            diag[r] = (up, send(DB.at[ahead], DB.at[ahead], ZM) if r < 4 else None)
        elif r == 5:
            diag[4][0].wait_recv()
            DR[...] = jnp.sum(DB[...], axis=0) * (1.0 / COLS)
        elif r == 6:
            rows = lax.broadcasted_iota(jnp.int32, (32, BLOCK), 0) + (z * 64 + y * 32)
            lanes = lax.broadcasted_iota(jnp.int32, (32, BLOCK), 1)
            G[z, y, :, 0:BLOCK] = jnp.where(rows == lanes, DR[0:1].astype(BF16), G[z, y, :, 0:BLOCK])

    plan = [gram, stage1, stage2, stage3, stage4, stage5]
    for r in range(START[-1] + 5):
        if r >= 1:
            diag_step(r)
        for t in range(TICKS):
            n = r - START[t] + (1 if t >= 6 and r > START[t] else 0)
            if 1 <= n <= 5:
                plan[n](t)
        for t in range(TICKS):
            if r == START[t]:
                gram(t)
        if r == 9:
            pass_hop(0)
            pass_hop(2)

    sent_y, served, hops, hops_pair = {}, {}, {}, {}

    def unit(q):
        u = zi(q)
        return u, lax.div(u, 2), lax.rem(u, 2)

    def products(qs):
        n = len(qs)

        def body(t, _):
            lanes = pl.ds(pl.multiple_of(t * BLOCK, BLOCK), BLOCK)
            left = jnp.concatenate([G[zi(q), :, :, lanes].reshape(UNIT, BLOCK) for q in qs], axis=0)
            p = dot(left, N[t].reshape(BLOCK, WIDTH), 0)

            @pl.when(t == 0)
            def _():
                YA[0 : UNIT * n] = p

            @pl.when(t > 0)
            def _():
                YA[0 : UNIT * n] += p

            return 0

        lax.fori_loop(0, TICKS, body, 0)
        for i, q in enumerate(qs):
            u, half, odd = unit(q)
            Y[0, u] = YA[UNIT * i : UNIT * (i + 1)].astype(BF16)
            sent_y[q] = (
                send(Y.at[0, u], Y.at[2 + half, odd], XP),
                send(Y.at[0, u], Y.at[2 + half, 4 + odd], XM),
                send(Y.at[0, u], Y.at[1, u], CP),
            )
        for i, q in enumerate(qs):
            u = zi(q)
            rows = G[u].reshape(UNIT, ROWS).astype(F32)
            square = jnp.sum(rows * rows, axis=1, keepdims=True)
            here = lax.broadcasted_iota(jnp.int32, (UNIT, BLOCK), 0) + u * UNIT
            lanes = lax.broadcasted_iota(jnp.int32, (UNIT, BLOCK), 1)
            g = jnp.sum(jnp.where(here == lanes, DR[0:1], 0.0), axis=1, keepdims=True)
            half = g.astype(BF16).astype(F32)
            poly = (cubic_coef * g + quintic_coef * square).astype(BF16).astype(F32)
            fix = poly - (cubic_coef * half + quintic_coef * square)
            X[u] = linear_coef * X[u] + cubic_coef * YA[UNIT * i : UNIT * (i + 1)] + fix * N[0, u].astype(F32)

    def serve(qs):
        for q in qs:
            u, half, odd = unit(q)
            sent_y[q][0].wait_recv()
            if q in (0, 1, 2, 3):
                hops[q] = send(Y.at[2 + half, odd], Y.at[6, u], XP)
            a = send(Y.at[2 + half, odd], Y.at[2 + half, 2 + odd], CP)
            sent_y[q][1].wait_recv()
            if q not in (0, 1, 2, 3):
                hops[q] = send(Y.at[2 + half, 4 + odd], Y.at[6, u], XM)
            b = send(Y.at[2 + half, 4 + odd], Y.at[2 + half, 6 + odd], CP)
            served[q] = (a, b)

    def pass_y(qs):
        for q in qs:
            hops[q].wait_recv()
            u = zi(q)
            hops_pair[q] = send(Y.at[6, u], Y.at[7, u], CP)

    wide, thin = pl.ds(SPLIT, ROWS - SPLIT), pl.ds(0, SPLIT)
    half_own = (pl.ds(0, ROWS // 2), pl.ds(ROWS // 2, ROWS // 2))
    half_thin = (pl.ds(0, SPLIT // 2), pl.ds(SPLIT // 2, SPLIT // 2))
    own, theirs, to_y = {}, {}, {}

    def rows_to(q, rows, part, peer):
        ref = G.at[zi(q), rows, :, part]
        return send(ref, ref, peer)

    def take_own(k):
        for part in (0, 1):
            for way, q, peer in ((0, -k, ZP), (1, k, ZM)):
                if k < 4 or part == way:
                    own[k, part, way].wait_recv()
                if k < 3 or (k == 3 and part == way):
                    own[k + 1, part, way] = rows_to(q, y, half_own[part], peer)
        for q in (-k, k) if k < 4 else (4,):
            to_y[q] = rows_to(q, y, wide, YP)

    def take_theirs(k):
        for way, q, peer in ((0, -k, ZP), (1, k, ZM)):
            theirs[k, way].wait_recv()
            if k < 3:
                theirs[k + 1, way] = rows_to(q, other, thin, peer)
            elif k == 3:
                theirs[k + 1, way] = rows_to(q, other, half_thin[way], peer)

    thin_y = rows_to(0, y, thin, YP)
    for part in (0, 1):
        for way, peer in ((0, ZP), (1, ZM)):
            own[1, part, way] = rows_to(0, y, half_own[part], peer)
    to_y[0] = rows_to(0, y, wide, YP)
    thin_y.wait_recv()
    for way, peer in ((0, ZP), (1, ZM)):
        theirs[1, way] = rows_to(0, other, thin, peer)
    pass_hop(1)
    pass_hop(3)
    take_own(1)
    for i in range(4):
        hop_pair[i].wait_recv()

    done = []
    for k in range(5):
        qs = [0] if k == 0 else [-k, k] if k < 4 else [4]
        if 1 <= k < 4:
            take_own(k + 1)
        for q in qs:
            to_y[q].wait_recv()
        products(qs)
        if k < 4:
            take_theirs(k + 1)
        if k >= 1:
            serve(done[-1])
        if k >= 2:
            pass_y(done[-2])
        done.append(qs)

    def add_up(t, m):
        left = G[4 * m : 4 * m + 4, :, :, BLOCK * t : BLOCK * (t + 1)].reshape(256, BLOCK)
        p = dot(left, Y[t].reshape(BLOCK, WIDTH), 0)
        X[4 * m : 4 * m + 4] += quintic_coef * p.reshape(4, UNIT, WIDTH)

    for q in sent_y:
        sent_y[q][2].wait_recv()
    for t in (0, 1):
        for m in range(2):
            add_up(t, m)
    serve([4])
    pass_y([-3, 3])
    for q in served:
        served[q][0].wait_recv()
        served[q][1].wait_recv()
    for t in (2, 3, 4, 5):
        for m in range(2):
            add_up(t, m)
    pass_y([4])
    for m in range(2):
        add_up(6, m)
    for q in hops_pair:
        hops_pair[q].wait_recv()
    stores = []
    for m in range(2):
        add_up(7, m)
        for u in range(4 * m, 4 * m + 4):
            stores.append(pltpu.make_async_copy(X.at[u], o_ref.at[pl.ds(UNIT * u, UNIT)], lsem.at[u]))
            stores[-1].start()
    for copy in started[-SENDS:]:
        copy.wait_send()
    for store in stores:
        store.wait()


def shards(iterate):
    scratch = [
        pltpu.VMEM((8, UNIT, WIDTH), F32),
        pltpu.VMEM((TICKS, 8, UNIT, WIDTH), BF16),
        pltpu.VMEM((TICKS, 8, UNIT, WIDTH), BF16),
        pltpu.VMEM((TICKS, 8, 128, 256), F32),
        pltpu.VMEM((8, 2, 32, ROWS), BF16),
        pltpu.VMEM((TICKS, 2, 128, 256), BF16),
        pltpu.VMEM((TICKS, 2, 128, 256), BF16),
        pltpu.VMEM((TICKS, 2, 128, 128), BF16),
        pltpu.VMEM((TICKS, 2, 128, 128), BF16),
        pltpu.VMEM((TICKS, 2, 128, 256), BF16),
        pltpu.VMEM((TICKS, 2, 128, 256), BF16),
        pltpu.VMEM((TICKS, 2, 128, 256), BF16),
        pltpu.VMEM((TICKS, 2, 64, 256), BF16),
        pltpu.VMEM((TICKS, 2, 64, 256), BF16),
        pltpu.VMEM((6, 8, 32, 256), BF16),
        pltpu.VMEM((6, 8, 32, 256), BF16),
        pltpu.VMEM((TICKS, 64, 256), BF16),
        pltpu.VMEM((TICKS, 64, 256), BF16),
        pltpu.VMEM((2, 32, BLOCK), BF16),
        pltpu.VMEM((8, BLOCK), F32),
        pltpu.VMEM((8, BLOCK), F32),
        pltpu.VMEM((8, 8, BLOCK), F32),
        pltpu.VMEM((2 * UNIT, WIDTH), F32),
        pltpu.SemaphoreType.DMA((MESSAGES,)),
        pltpu.SemaphoreType.DMA((MESSAGES,)),
        pltpu.SemaphoreType.DMA((8,)),
    ]
    return pl.pallas_call(
        kernel,
        out_shape=jax.ShapeDtypeStruct(iterate.shape, F32),
        in_specs=[pl.BlockSpec(memory_space=pl.ANY)],
        out_specs=pl.BlockSpec(memory_space=pl.ANY),
        scratch_shapes=scratch,
        compiler_params=pltpu.CompilerParams(
            collective_id=0, has_side_effects=True, vmem_limit_bytes=60 * 1024 * 1024
        ),
        cost_estimate=pl.CostEstimate(flops=6 * BLOCK * ROWS * WIDTH, bytes_accessed=8 * BLOCK * WIDTH, transcendentals=0),
    )(iterate)


def solution(mesh):
    return jax.shard_map(
        shards,
        mesh=mesh,
        in_specs=(P(("mat", "band"), "col"),),
        out_specs=P(("mat", "band"), "col"),
        check_vma=False,
    )
```

```python
import jax
import jax.numpy as jnp
from jax import lax
from jax.experimental import pallas as pl
from jax.experimental.pallas import tpu as pltpu
from jax.sharding import PartitionSpec as P

COLS = 18432
MESH = pl.DeviceIdType.MESH
linear_coef = 3.4445
cubic_coef = -4.775
quintic_coef = 2.0315

F32, BF16 = jnp.float32, jnp.bfloat16
BLOCK, WIDTH, TICKS, UNIT = 512, 1152, 8, 64
ROWS = BLOCK * TICKS
SPLIT = 1536
MESSAGES, SENDS = 222, 48
START = (0, 1, 2, 3, 4, 5, 5, 5)
FLIGHT = 4


def dot(a, b, contract):
    return lax.dot_general(a, b, (((1,), (contract,)), ((), ())), preferred_element_type=F32)


def kernel(x_ref, o_ref, X, N, Y, V, G, SA, RA, SH, RH, SB, RB, SC, RC, RD, YS, YR, FS, FR, GS, DS, DR, DB, YA, ssem, rsem, lsem):
    mat, band, col = lax.axis_index("mat"), lax.axis_index("band"), lax.axis_index("col")
    x, core = lax.div(band, 2), lax.rem(band, 2)
    z, y = lax.div(col, 2), lax.rem(col, 2)
    other = 1 - y

    def at_x(d):
        return (mat, lax.rem(x + d + 4, 4) * 2 + core, col)

    def zi(d):
        return lax.rem(z + d + 8, 8)

    def at_z(d):
        return (mat, band, zi(d) * 2 + y)

    XP, XM, ZP, ZM, ZPP, ZMM = at_x(1), at_x(-1), at_z(1), at_z(-1), at_z(2), at_z(-2)
    YP = (mat, band, z * 2 + other)
    ZPY, ZMY = (mat, band, zi(1) * 2 + other), (mat, band, zi(-1) * 2 + other)
    CP = (mat, x * 2 + 1 - core, col)

    started = []

    def send(src, dst, peer):
        n = len(started)
        if n >= SENDS:
            started[n - SENDS].wait_send()
        copy = pltpu.make_async_remote_copy(
            src_ref=src,
            dst_ref=dst,
            send_sem=ssem.at[n % SENDS],
            recv_sem=rsem.at[n],
            device_id=peer,
            device_id_type=MESH,
        )
        copy.start()
        started.append(copy)
        return copy

    loads = [pltpu.make_async_copy(x_ref.at[pl.ds(UNIT * u, UNIT)], X.at[u], lsem.at[u]) for u in range(8)]
    for load in loads:
        load.start()
    barrier = pltpu.get_barrier_semaphore()
    for peer in (XP, XM, ZP, ZM, ZPP, ZMM, ZPY, ZMY, YP, CP):
        pl.semaphore_signal(barrier, inc=1, device_id=peer, device_id_type=MESH)
    for u, load in enumerate(loads):
        load.wait()
        N[0, u] = X[u].astype(BF16)
    pl.semaphore_wait(barrier, 10)

    plus, minus, pair, hop, hop_pair = {}, {}, {}, {}, {}
    relay = {}

    def send_own(i):
        plus[i] = send(N.at[0, pl.ds(2 * i, 2)], N.at[2 + i, pl.ds(0, 2)], XP)
        minus[i] = send(N.at[0, pl.ds(2 * i, 2)], N.at[2 + i, pl.ds(4, 2)], XM)

    def send_hop(i):
        if i < 2:
            hop[i] = send(N.at[2 + i, pl.ds(0, 2)], N.at[6, pl.ds(2 * i, 2)], XP)
        else:
            hop[i] = send(N.at[2 + i, pl.ds(4, 2)], N.at[6, pl.ds(2 * i, 2)], XM)

    def pass_hop(i):
        hop[i].wait_recv()
        hop_pair[i] = send(N.at[6, pl.ds(2 * i, 2)], N.at[7, pl.ds(2 * i, 2)], CP)

    send_own(0)
    pair_block = send(N.at[0], N.at[1], CP)
    for i in range(1, FLIGHT):
        send_own(i)

    def arrive(t):
        if t == 1:
            pair_block.wait_recv()
        if 2 <= t <= 5:
            i = t - 2
            plus[i].wait_recv()
            relay[i, 0] = send(N.at[t, pl.ds(0, 2)], N.at[t, pl.ds(2, 2)], CP)
            minus[i].wait_recv()
            relay[i, 1] = send(N.at[t, pl.ds(4, 2)], N.at[t, pl.ds(6, 2)], CP)
            if i + FLIGHT < 4:
                send_own(i + FLIGHT)
            if i >= 2:
                send_hop(i - 2)
                send_hop(i)
            relay[i, 0].wait_recv()
            relay[i, 1].wait_recv()

    first, own_part, ring1, ring2, ring3, moved, diag = {}, {}, {}, {}, {}, {}, {}

    def height(t):
        return 96 if t < 6 else 128

    def gram(t):
        arrive(t)
        if t <= 5:
            right = N[t].reshape(BLOCK, WIDTH)
        elif t == 6:
            right = N[2:6, 4:6].reshape(BLOCK, WIDTH)
        else:
            right = N[2:6, 2:4].reshape(BLOCK, WIDTH)
        total = jnp.zeros((1, BLOCK), F32)
        for m in range(2):
            if t <= 5:
                left = N[0, 4 * m : 4 * m + 4].reshape(256, WIDTH)
            elif t == 6:
                left = N[2 + 2 * m : 4 + 2 * m, 0:2].reshape(256, WIDTH)
            else:
                left = N[2 + 2 * m : 4 + 2 * m, 4:6].reshape(256, WIDTH)
            p = dot(left, right, 1)
            if t == 0:
                rows = lax.broadcasted_iota(jnp.int32, (256, BLOCK), 0) + 256 * m
                lanes = lax.broadcasted_iota(jnp.int32, (256, BLOCK), 1)
                total += jnp.sum(jnp.where(rows == lanes, p, 0.0), axis=0, keepdims=True)
            p = p.reshape(4, UNIT, BLOCK)
            low, high = p[:, 0:32], p[:, 32:64]
            mine, rest = jnp.where(y == 0, low, high), jnp.where(y == 0, high, low)
            here = pl.ds(4 * m, 4)
            V[t, here, 0:32, :] = mine[:, :, 0:256]
            V[t, here, 32:64, :] = mine[:, :, 256:]
            V[t, here, 64:96, :] = rest[:, :, 0:256]
            if t < 6:
                YS[t, here] = rest[:, :, 256:].astype(BF16)
            else:
                V[t, here, 96:128, :] = rest[:, :, 256:]
        if t < 6:
            first[t] = send(YS.at[t], YR.at[t], YP)
        else:
            launch(t)
        if t == 0:
            DS[...] = jnp.broadcast_to(total, (8, BLOCK))
            diag["y"] = send(DS, DR, YP)

    def stage1(t):
        if t < 6:
            first[t].wait_recv()
            V[t, :, 32:64, :] += YR[t].astype(F32)
            launch(t)

    def launch(t):
        h = height(t)
        sent = []
        for way, peer, far in ((0, ZP, ZPP), (1, ZM, ZMM)):
            d = zi(3) if way == 0 else zi(-3)
            SA[t, way, 0:h] = V[t, d, 0:h].astype(BF16)
            sent.append(send(SA.at[t, way, pl.ds(0, h)], RA.at[t, way, pl.ds(0, h)], peer))
            SH[t, way, 0:h] = V[t, zi(4), 0:h, 128 * way : 128 * way + 128].astype(BF16)
            sent.append(send(SH.at[t, way, pl.ds(0, h)], RH.at[t, way, pl.ds(0, h)], far))
        ring1[t] = sent
        FS[t, 0 : h - 64] = V[t, z, 64:h].astype(BF16)
        own_part[t] = send(FS.at[t, pl.ds(0, h - 64)], FR.at[t, pl.ds(0, h - 64)], YP)

    def stage2(t):
        h = height(t)
        sent = []
        for way, peer in ((0, ZP), (1, ZM)):
            ring1[t][2 * way].wait_recv()
            ring1[t][2 * way + 1].wait_recv()
            d = zi(2) if way == 0 else zi(-2)
            half, rest = pl.ds(128 * way, 128), pl.ds(128 - 128 * way, 128)
            SB[t, way, 0:h, half] = (
                V[t, d, 0:h, half] + RA[t, way, 0:h, half].astype(F32) + RH[t, way, 0:h].astype(F32)
            ).astype(BF16)
            SB[t, way, 0:h, rest] = (V[t, d, 0:h, rest] + RA[t, way, 0:h, rest].astype(F32)).astype(BF16)
            sent.append(send(SB.at[t, way, pl.ds(0, h)], RB.at[t, way, pl.ds(0, h)], peer))
        ring2[t] = sent

    def stage3(t):
        h = height(t)
        sent = []
        for way, peer, across in ((0, ZP, ZPY), (1, ZM, ZMY)):
            ring2[t][way].wait_recv()
            d = zi(1) if way == 0 else zi(-1)
            SC[t, way, 0:h] = (V[t, d, 0:h] + RB[t, way, 0:h].astype(F32)).astype(BF16)
            sent.append(send(SC.at[t, way, pl.ds(0, 64)], RC.at[t, way], peer))
            sent.append(send(SC.at[t, way, pl.ds(64, h - 64)], RD.at[t, way, pl.ds(0, h - 64)], across))
        ring3[t] = sent

    early = {}

    def tell(t):
        ref = G.at[z, y, :, pl.ds(BLOCK * t, BLOCK)]
        early[t] = send(ref, ref, YP)

    def stage4(t):
        for copy in ring3[t]:
            copy.wait_recv()
        own_part[t].wait_recv()
        r = V[t, z, 0:64] + RC[t, 0].astype(F32) + RC[t, 1].astype(F32)
        n = height(t) - 64
        cross = RD[t, 0, 0:n].astype(F32) + RD[t, 1, 0:n].astype(F32) + FR[t, 0:n].astype(F32)
        low, high = r[0:32] + cross[0:32], r[32:64]
        if n == 64:
            high = high + cross[32:64]
        g = (jnp.concatenate([low, high], axis=1) * (1.0 / COLS)).astype(BF16)
        if t < 6:
            G[z, y, :, BLOCK * t : BLOCK * (t + 1)] = g
            if t > 0:
                tell(t)
        else:
            GS[t - 6] = g
            there = G.at[z, y, :, pl.ds(BLOCK * t, BLOCK)]
            moved[t] = send(GS.at[t - 6], there, XM if t == 6 else XP)

    def stage5(t):
        if t >= 6:
            moved[t].wait_recv()
            tell(t)

    def diag_step(r):
        if r == 1:
            diag["y"].wait_recv()
            DB[z] = DS[...] + DR[...]
            diag[1] = (send(DB.at[z], DB.at[z], ZP), send(DB.at[z], DB.at[z], ZM))
        elif r <= 4:
            diag[r - 1][0].wait_recv()
            back = zi(1 - r)
            up = send(DB.at[back], DB.at[back], ZP)
            diag[r - 1][1].wait_recv()
            ahead = zi(r - 1)
            diag[r] = (up, send(DB.at[ahead], DB.at[ahead], ZM) if r < 4 else None)
        elif r == 5:
            diag[4][0].wait_recv()
            DR[...] = jnp.sum(DB[...], axis=0) * (1.0 / COLS)
        elif r == 6:
            rows = lax.broadcasted_iota(jnp.int32, (32, BLOCK), 0) + (z * 64 + y * 32)
            lanes = lax.broadcasted_iota(jnp.int32, (32, BLOCK), 1)
            G[z, y, :, 0:BLOCK] = jnp.where(rows == lanes, DR[0:1].astype(BF16), G[z, y, :, 0:BLOCK])
            tell(0)

    wide, thin = pl.ds(SPLIT, ROWS - SPLIT), pl.ds(0, SPLIT)
    half_own = (pl.ds(0, ROWS // 2), pl.ds(ROWS // 2, ROWS // 2))
    half_thin = (pl.ds(0, SPLIT // 2), pl.ds(SPLIT // 2, SPLIT // 2))
    own, theirs, to_y = {}, {}, {}

    def rows_to(q, rows, part, peer):
        ref = G.at[zi(q), rows, :, part]
        return send(ref, ref, peer)

    plan = [gram, stage1, stage2, stage3, stage4, stage5]
    for r in range(START[-1] + 5):
        if r >= 1:
            diag_step(r)
        for t in range(TICKS):
            n = r - START[t] + (1 if t >= 6 and r > START[t] else 0)
            if 1 <= n <= 5:
                plan[n](t)
        for t in range(TICKS):
            if r == START[t]:
                gram(t)
        if r == START[-1] + 3:
            for way, peer in ((0, ZP), (1, ZM)):
                own[1, 0, way] = rows_to(0, y, half_own[0], peer)
            for t in (0, 1, 2):
                early[t].wait_recv()
            for way, peer in ((0, ZP), (1, ZM)):
                theirs[1, way] = rows_to(0, other, thin, peer)

    sent_y, served, hops, hops_pair = {}, {}, {}, {}

    def unit(q):
        u = zi(q)
        return u, lax.div(u, 2), lax.rem(u, 2)

    def products(qs):
        n = len(qs)

        def body(t, _):
            lanes = pl.ds(pl.multiple_of(t * BLOCK, BLOCK), BLOCK)
            left = jnp.concatenate([G[zi(q), :, :, lanes].reshape(UNIT, BLOCK) for q in qs], axis=0)
            p = dot(left, N[t].reshape(BLOCK, WIDTH), 0)

            @pl.when(t == 0)
            def _():
                YA[0 : UNIT * n] = p

            @pl.when(t > 0)
            def _():
                YA[0 : UNIT * n] += p

            return 0

        lax.fori_loop(0, TICKS, body, 0)
        for i, q in enumerate(qs):
            u, half, odd = unit(q)
            Y[0, u] = YA[UNIT * i : UNIT * (i + 1)].astype(BF16)
            sent_y[q] = (
                send(Y.at[0, u], Y.at[2 + half, odd], XP),
                send(Y.at[0, u], Y.at[2 + half, 4 + odd], XM),
                send(Y.at[0, u], Y.at[1, u], CP),
            )
        for i, q in enumerate(qs):
            u = zi(q)
            rows = G[u].reshape(UNIT, ROWS).astype(F32)
            square = jnp.sum(rows * rows, axis=1, keepdims=True)
            here = lax.broadcasted_iota(jnp.int32, (UNIT, BLOCK), 0) + u * UNIT
            lanes = lax.broadcasted_iota(jnp.int32, (UNIT, BLOCK), 1)
            g = jnp.sum(jnp.where(here == lanes, DR[0:1], 0.0), axis=1, keepdims=True)
            half = g.astype(BF16).astype(F32)
            poly = (cubic_coef * g + quintic_coef * square).astype(BF16).astype(F32)
            fix = poly - (cubic_coef * half + quintic_coef * square)
            X[u] = linear_coef * X[u] + cubic_coef * YA[UNIT * i : UNIT * (i + 1)] + fix * N[0, u].astype(F32)

    def serve(qs):
        for q in qs:
            u, half, odd = unit(q)
            sent_y[q][0].wait_recv()
            if q in (0, 1, 2, 3):
                hops[q] = send(Y.at[2 + half, odd], Y.at[6, u], XP)
            a = send(Y.at[2 + half, odd], Y.at[2 + half, 2 + odd], CP)
            sent_y[q][1].wait_recv()
            if q not in (0, 1, 2, 3):
                hops[q] = send(Y.at[2 + half, 4 + odd], Y.at[6, u], XM)
            b = send(Y.at[2 + half, 4 + odd], Y.at[2 + half, 6 + odd], CP)
            served[q] = (a, b)

    def pass_y(qs):
        for q in qs:
            hops[q].wait_recv()
            u = zi(q)
            hops_pair[q] = send(Y.at[6, u], Y.at[7, u], CP)

    def take_own(k):
        for part in (0, 1):
            for way, q, peer in ((0, -k, ZP), (1, k, ZM)):
                if k < 4 or part == way:
                    own[k, part, way].wait_recv()
                if k < 3 or (k == 3 and part == way):
                    own[k + 1, part, way] = rows_to(q, y, half_own[part], peer)
        for q in (-k, k) if k < 4 else (4,):
            to_y[q] = rows_to(q, y, wide, YP)

    def take_theirs(k):
        for way, q, peer in ((0, -k, ZP), (1, k, ZM)):
            theirs[k, way].wait_recv()
            if k < 3:
                theirs[k + 1, way] = rows_to(q, other, thin, peer)
            elif k == 3:
                theirs[k + 1, way] = rows_to(q, other, half_thin[way], peer)

    for way, peer in ((0, ZP), (1, ZM)):
        own[1, 1, way] = rows_to(0, y, half_own[1], peer)
    for i in (0, 2, 1, 3):
        pass_hop(i)
    for t in range(3, TICKS):
        early[t].wait_recv()
    for i in range(4):
        hop_pair[i].wait_recv()

    done = []
    for k in range(5):
        qs = [0] if k == 0 else [-k, k] if k < 4 else [4]
        if k < 4:
            take_own(k + 1)
        if k >= 1:
            for q in qs:
                to_y[q].wait_recv()
        products(qs)
        if k >= 1:
            serve(done[-1])
        if k < 4:
            take_theirs(k + 1)
        if k >= 2:
            pass_y(done[-2])
        done.append(qs)

    def add_up(t, m):
        left = G[4 * m : 4 * m + 4, :, :, BLOCK * t : BLOCK * (t + 1)].reshape(256, BLOCK)
        p = dot(left, Y[t].reshape(BLOCK, WIDTH), 0)
        X[4 * m : 4 * m + 4] += quintic_coef * p.reshape(4, UNIT, WIDTH)

    for q in sent_y:
        sent_y[q][2].wait_recv()
    for t in (0, 1):
        for m in range(2):
            add_up(t, m)
    serve([4])
    pass_y([-3, 3])
    for q in served:
        served[q][0].wait_recv()
        served[q][1].wait_recv()
    for t in (2, 3, 4, 5):
        for m in range(2):
            add_up(t, m)
    pass_y([4])
    for m in range(2):
        add_up(6, m)
    for q in hops_pair:
        hops_pair[q].wait_recv()
    stores = []
    for m in range(2):
        add_up(7, m)
        for u in range(4 * m, 4 * m + 4):
            stores.append(pltpu.make_async_copy(X.at[u], o_ref.at[pl.ds(UNIT * u, UNIT)], lsem.at[u]))
            stores[-1].start()
    for copy in started[-SENDS:]:
        copy.wait_send()
    for store in stores:
        store.wait()


def shards(iterate):
    scratch = [
        pltpu.VMEM((8, UNIT, WIDTH), F32),
        pltpu.VMEM((TICKS, 8, UNIT, WIDTH), BF16),
        pltpu.VMEM((TICKS, 8, UNIT, WIDTH), BF16),
        pltpu.VMEM((TICKS, 8, 128, 256), F32),
        pltpu.VMEM((8, 2, 32, ROWS), BF16),
        pltpu.VMEM((TICKS, 2, 128, 256), BF16),
        pltpu.VMEM((TICKS, 2, 128, 256), BF16),
        pltpu.VMEM((TICKS, 2, 128, 128), BF16),
        pltpu.VMEM((TICKS, 2, 128, 128), BF16),
        pltpu.VMEM((TICKS, 2, 128, 256), BF16),
        pltpu.VMEM((TICKS, 2, 128, 256), BF16),
        pltpu.VMEM((TICKS, 2, 128, 256), BF16),
        pltpu.VMEM((TICKS, 2, 64, 256), BF16),
        pltpu.VMEM((TICKS, 2, 64, 256), BF16),
        pltpu.VMEM((6, 8, 32, 256), BF16),
        pltpu.VMEM((6, 8, 32, 256), BF16),
        pltpu.VMEM((TICKS, 64, 256), BF16),
        pltpu.VMEM((TICKS, 64, 256), BF16),
        pltpu.VMEM((2, 32, BLOCK), BF16),
        pltpu.VMEM((8, BLOCK), F32),
        pltpu.VMEM((8, BLOCK), F32),
        pltpu.VMEM((8, 8, BLOCK), F32),
        pltpu.VMEM((2 * UNIT, WIDTH), F32),
        pltpu.SemaphoreType.DMA((MESSAGES,)),
        pltpu.SemaphoreType.DMA((MESSAGES,)),
        pltpu.SemaphoreType.DMA((8,)),
    ]
    return pl.pallas_call(
        kernel,
        out_shape=jax.ShapeDtypeStruct(iterate.shape, F32),
        in_specs=[pl.BlockSpec(memory_space=pl.ANY)],
        out_specs=pl.BlockSpec(memory_space=pl.ANY),
        scratch_shapes=scratch,
        compiler_params=pltpu.CompilerParams(
            collective_id=0, has_side_effects=True, vmem_limit_bytes=60 * 1024 * 1024
        ),
        cost_estimate=pl.CostEstimate(flops=6 * BLOCK * ROWS * WIDTH, bytes_accessed=8 * BLOCK * WIDTH, transcendentals=0),
    )(iterate)


def solution(mesh):
    return jax.shard_map(
        shards,
        mesh=mesh,
        in_specs=(P(("mat", "band"), "col"),),
        out_specs=P(("mat", "band"), "col"),
        check_vma=False,
    )
```

```python
import jax
import jax.numpy as jnp
from jax import lax
from jax.experimental import pallas as pl
from jax.experimental.pallas import tpu as pltpu
from jax.sharding import PartitionSpec as P

COLS = 18432
MESH = pl.DeviceIdType.MESH
linear_coef = 3.4445
cubic_coef = -4.775
quintic_coef = 2.0315

F32, BF16 = jnp.float32, jnp.bfloat16
BLOCK, WIDTH, TICKS, UNIT = 512, 1152, 8, 64
ROWS = BLOCK * TICKS
SPLIT = 1536
MESSAGES, SENDS = 222, 48
START = (0, 1, 2, 3, 4, 5, 5, 5)
FLIGHT = 4


def dot(a, b, contract):
    return lax.dot_general(a, b, (((1,), (contract,)), ((), ())), preferred_element_type=F32)


def kernel(x_ref, o_ref, X, N, Y, V, G, SA, RA, SH, RH, SB, RB, SC, RC, RD, YS, YR, FS, FR, GS, DS, DR, DB, YA, ssem, rsem, lsem):
    mat, band, col = lax.axis_index("mat"), lax.axis_index("band"), lax.axis_index("col")
    x, core = lax.div(band, 2), lax.rem(band, 2)
    z, y = lax.div(col, 2), lax.rem(col, 2)
    other = 1 - y

    def at_x(d):
        return (mat, lax.rem(x + d + 4, 4) * 2 + core, col)

    def zi(d):
        return lax.rem(z + d + 8, 8)

    def at_z(d):
        return (mat, band, zi(d) * 2 + y)

    XP, XM, ZP, ZM, ZPP, ZMM = at_x(1), at_x(-1), at_z(1), at_z(-1), at_z(2), at_z(-2)
    YP = (mat, band, z * 2 + other)
    ZPY, ZMY = (mat, band, zi(1) * 2 + other), (mat, band, zi(-1) * 2 + other)
    CP = (mat, x * 2 + 1 - core, col)

    started = []

    def send(src, dst, peer):
        n = len(started)
        if n >= SENDS:
            started[n - SENDS].wait_send()
        copy = pltpu.make_async_remote_copy(
            src_ref=src,
            dst_ref=dst,
            send_sem=ssem.at[n % SENDS],
            recv_sem=rsem.at[n],
            device_id=peer,
            device_id_type=MESH,
        )
        copy.start()
        started.append(copy)
        return copy

    loads = [pltpu.make_async_copy(x_ref.at[pl.ds(UNIT * u, UNIT)], X.at[u], lsem.at[u]) for u in range(8)]
    for load in loads:
        load.start()
    barrier = pltpu.get_barrier_semaphore()
    for peer in (XP, XM, ZP, ZM, ZPP, ZMM, ZPY, ZMY, YP, CP):
        pl.semaphore_signal(barrier, inc=1, device_id=peer, device_id_type=MESH)
    for u, load in enumerate(loads):
        load.wait()
        N[0, u] = X[u].astype(BF16)
    pl.semaphore_wait(barrier, 10)

    plus, minus, pair, hop, hop_pair = {}, {}, {}, {}, {}
    relay = {}

    def send_own(i):
        plus[i] = send(N.at[0, pl.ds(2 * i, 2)], N.at[2 + i, pl.ds(0, 2)], XP)
        minus[i] = send(N.at[0, pl.ds(2 * i, 2)], N.at[2 + i, pl.ds(4, 2)], XM)

    def send_hop(i):
        if i < 2:
            hop[i] = send(N.at[2 + i, pl.ds(0, 2)], N.at[6, pl.ds(2 * i, 2)], XP)
        else:
            hop[i] = send(N.at[2 + i, pl.ds(4, 2)], N.at[6, pl.ds(2 * i, 2)], XM)

    def pass_hop(i):
        hop[i].wait_recv()
        hop_pair[i] = send(N.at[6, pl.ds(2 * i, 2)], N.at[7, pl.ds(2 * i, 2)], CP)

    send_own(0)
    pair_block = send(N.at[0], N.at[1], CP)
    for i in range(1, FLIGHT):
        send_own(i)

    def arrive(t):
        if t == 1:
            pair_block.wait_recv()
        if 2 <= t <= 5:
            i = t - 2
            plus[i].wait_recv()
            relay[i, 0] = send(N.at[t, pl.ds(0, 2)], N.at[t, pl.ds(2, 2)], CP)
            minus[i].wait_recv()
            relay[i, 1] = send(N.at[t, pl.ds(4, 2)], N.at[t, pl.ds(6, 2)], CP)
            if i + FLIGHT < 4:
                send_own(i + FLIGHT)
            if i >= 2:
                send_hop(i - 2)
                send_hop(i)
            relay[i, 0].wait_recv()
            relay[i, 1].wait_recv()

    first, own_part, ring1, ring2, ring3, moved, diag = {}, {}, {}, {}, {}, {}, {}

    def height(t):
        return 96 if t < 6 else 128

    def gram(t):
        arrive(t)
        if t <= 5:
            right = N[t].reshape(BLOCK, WIDTH)
        elif t == 6:
            right = N[2:6, 4:6].reshape(BLOCK, WIDTH)
        else:
            right = N[2:6, 2:4].reshape(BLOCK, WIDTH)
        total = jnp.zeros((1, BLOCK), F32)
        for m in range(2):
            if t <= 5:
                left = N[0, 4 * m : 4 * m + 4].reshape(256, WIDTH)
            elif t == 6:
                left = N[2 + 2 * m : 4 + 2 * m, 0:2].reshape(256, WIDTH)
            else:
                left = N[2 + 2 * m : 4 + 2 * m, 4:6].reshape(256, WIDTH)
            p = dot(left, right, 1)
            if t == 0:
                rows = lax.broadcasted_iota(jnp.int32, (256, BLOCK), 0) + 256 * m
                lanes = lax.broadcasted_iota(jnp.int32, (256, BLOCK), 1)
                total += jnp.sum(jnp.where(rows == lanes, p, 0.0), axis=0, keepdims=True)
            p = p.reshape(4, UNIT, BLOCK)
            low, high = p[:, 0:32], p[:, 32:64]
            mine, rest = jnp.where(y == 0, low, high), jnp.where(y == 0, high, low)
            here = pl.ds(4 * m, 4)
            V[t, here, 0:32, :] = mine[:, :, 0:256]
            V[t, here, 32:64, :] = mine[:, :, 256:]
            V[t, here, 64:96, :] = rest[:, :, 0:256]
            if t < 6:
                YS[t, here] = rest[:, :, 256:].astype(BF16)
            else:
                V[t, here, 96:128, :] = rest[:, :, 256:]
        if t < 6:
            first[t] = send(YS.at[t], YR.at[t], YP)
        else:
            launch(t)
        if t == 0:
            DS[...] = jnp.broadcast_to(total, (8, BLOCK))
            diag["y"] = send(DS, DR, YP)

    def stage1(t):
        if t < 6:
            first[t].wait_recv()
            V[t, :, 32:64, :] += YR[t].astype(F32)
            launch(t)

    def launch(t):
        h = height(t)
        sent = []
        for way, peer, far in ((0, ZP, ZPP), (1, ZM, ZMM)):
            d = zi(3) if way == 0 else zi(-3)
            SA[t, way, 0:h] = V[t, d, 0:h].astype(BF16)
            sent.append(send(SA.at[t, way, pl.ds(0, h)], RA.at[t, way, pl.ds(0, h)], peer))
            SH[t, way, 0:h] = V[t, zi(4), 0:h, 128 * way : 128 * way + 128].astype(BF16)
            sent.append(send(SH.at[t, way, pl.ds(0, h)], RH.at[t, way, pl.ds(0, h)], far))
        ring1[t] = sent
        FS[t, 0 : h - 64] = V[t, z, 64:h].astype(BF16)
        own_part[t] = send(FS.at[t, pl.ds(0, h - 64)], FR.at[t, pl.ds(0, h - 64)], YP)

    def stage2(t):
        h = height(t)
        sent = []
        for way, peer in ((0, ZP), (1, ZM)):
            ring1[t][2 * way].wait_recv()
            ring1[t][2 * way + 1].wait_recv()
            d = zi(2) if way == 0 else zi(-2)
            half, rest = pl.ds(128 * way, 128), pl.ds(128 - 128 * way, 128)
            SB[t, way, 0:h, half] = (
                V[t, d, 0:h, half] + RA[t, way, 0:h, half].astype(F32) + RH[t, way, 0:h].astype(F32)
            ).astype(BF16)
            SB[t, way, 0:h, rest] = (V[t, d, 0:h, rest] + RA[t, way, 0:h, rest].astype(F32)).astype(BF16)
            sent.append(send(SB.at[t, way, pl.ds(0, h)], RB.at[t, way, pl.ds(0, h)], peer))
        ring2[t] = sent

    def stage3(t):
        h = height(t)
        sent = []
        for way, peer, across in ((0, ZP, ZPY), (1, ZM, ZMY)):
            ring2[t][way].wait_recv()
            d = zi(1) if way == 0 else zi(-1)
            SC[t, way, 0:h] = (V[t, d, 0:h] + RB[t, way, 0:h].astype(F32)).astype(BF16)
            sent.append(send(SC.at[t, way, pl.ds(0, 64)], RC.at[t, way], peer))
            sent.append(send(SC.at[t, way, pl.ds(64, h - 64)], RD.at[t, way, pl.ds(0, h - 64)], across))
        ring3[t] = sent

    early = {}

    def tell(t):
        ref = G.at[z, y, :, pl.ds(BLOCK * t, BLOCK)]
        early[t] = send(ref, ref, YP)

    def stage4(t):
        for copy in ring3[t]:
            copy.wait_recv()
        own_part[t].wait_recv()
        r = V[t, z, 0:64] + RC[t, 0].astype(F32) + RC[t, 1].astype(F32)
        n = height(t) - 64
        cross = RD[t, 0, 0:n].astype(F32) + RD[t, 1, 0:n].astype(F32) + FR[t, 0:n].astype(F32)
        low, high = r[0:32] + cross[0:32], r[32:64]
        if n == 64:
            high = high + cross[32:64]
        g = (jnp.concatenate([low, high], axis=1) * (1.0 / COLS)).astype(BF16)
        if t < 6:
            G[z, y, :, BLOCK * t : BLOCK * (t + 1)] = g
            if t > 0:
                tell(t)
        else:
            GS[t - 6] = g
            there = G.at[z, y, :, pl.ds(BLOCK * t, BLOCK)]
            moved[t] = send(GS.at[t - 6], there, XM if t == 6 else XP)

    def stage5(t):
        if t >= 6:
            moved[t].wait_recv()
            tell(t)

    def diag_step(r):
        if r == 1:
            diag["y"].wait_recv()
            DB[z] = DS[...] + DR[...]
            diag[1] = (send(DB.at[z], DB.at[z], ZP), send(DB.at[z], DB.at[z], ZM))
        elif r <= 4:
            diag[r - 1][0].wait_recv()
            back = zi(1 - r)
            up = send(DB.at[back], DB.at[back], ZP)
            diag[r - 1][1].wait_recv()
            ahead = zi(r - 1)
            diag[r] = (up, send(DB.at[ahead], DB.at[ahead], ZM) if r < 4 else None)
        elif r == 5:
            diag[4][0].wait_recv()
            DR[...] = jnp.sum(DB[...], axis=0) * (1.0 / COLS)
        elif r == 6:
            rows = lax.broadcasted_iota(jnp.int32, (32, BLOCK), 0) + (z * 64 + y * 32)
            lanes = lax.broadcasted_iota(jnp.int32, (32, BLOCK), 1)
            G[z, y, :, 0:BLOCK] = jnp.where(rows == lanes, DR[0:1].astype(BF16), G[z, y, :, 0:BLOCK])
            tell(0)

    wide, thin = pl.ds(SPLIT, ROWS - SPLIT), pl.ds(0, SPLIT)
    half_own = (pl.ds(0, ROWS // 2), pl.ds(ROWS // 2, ROWS // 2))
    half_thin = (pl.ds(0, SPLIT // 2), pl.ds(SPLIT // 2, SPLIT // 2))
    own, theirs, to_y = {}, {}, {}

    def rows_to(q, rows, part, peer):
        ref = G.at[zi(q), rows, :, part]
        return send(ref, ref, peer)

    plan = [gram, stage1, stage2, stage3, stage4, stage5]
    for r in range(START[-1] + 5):
        for t in range(TICKS) if r == START[-1] else ():
            if r == START[t]:
                gram(t)
        if r >= 1:
            diag_step(r)
        for t in reversed(range(TICKS)) if r > START[-1] else range(TICKS):
            n = r - START[t] + (1 if t >= 6 and r > START[t] else 0)
            if 1 <= n <= 5:
                plan[n](t)
        for t in range(TICKS):
            if r == START[t] and r < START[-1]:
                gram(t)
        if r == START[-1] + 3:
            for way, peer in ((0, ZP), (1, ZM)):
                own[1, 0, way] = rows_to(0, y, half_own[0], peer)
            for t in (0, 1, 2):
                early[t].wait_recv()
            for way, peer in ((0, ZP), (1, ZM)):
                theirs[1, way] = rows_to(0, other, thin, peer)

    sent_y, served, hops, hops_pair = {}, {}, {}, {}

    def unit(q):
        u = zi(q)
        return u, lax.div(u, 2), lax.rem(u, 2)

    def products(qs):
        n = len(qs)

        def body(t, _):
            lanes = pl.ds(pl.multiple_of(t * BLOCK, BLOCK), BLOCK)
            left = jnp.concatenate([G[zi(q), :, :, lanes].reshape(UNIT, BLOCK) for q in qs], axis=0)
            p = dot(left, N[t].reshape(BLOCK, WIDTH), 0)

            @pl.when(t == 0)
            def _():
                YA[0 : UNIT * n] = p

            @pl.when(t > 0)
            def _():
                YA[0 : UNIT * n] += p

            return 0

        lax.fori_loop(0, TICKS, body, 0)
        for i, q in enumerate(qs):
            u, half, odd = unit(q)
            Y[0, u] = YA[UNIT * i : UNIT * (i + 1)].astype(BF16)
            sent_y[q] = (
                send(Y.at[0, u], Y.at[2 + half, odd], XP),
                send(Y.at[0, u], Y.at[2 + half, 4 + odd], XM),
                send(Y.at[0, u], Y.at[1, u], CP),
            )
        for i, q in enumerate(qs):
            u = zi(q)
            rows = G[u].reshape(UNIT, ROWS).astype(F32)
            square = jnp.sum(rows * rows, axis=1, keepdims=True)
            here = lax.broadcasted_iota(jnp.int32, (UNIT, BLOCK), 0) + u * UNIT
            lanes = lax.broadcasted_iota(jnp.int32, (UNIT, BLOCK), 1)
            g = jnp.sum(jnp.where(here == lanes, DR[0:1], 0.0), axis=1, keepdims=True)
            half = g.astype(BF16).astype(F32)
            poly = (cubic_coef * g + quintic_coef * square).astype(BF16).astype(F32)
            fix = poly - (cubic_coef * half + quintic_coef * square)
            X[u] = linear_coef * X[u] + cubic_coef * YA[UNIT * i : UNIT * (i + 1)] + fix * N[0, u].astype(F32)

    def serve(qs):
        for q in qs:
            u, half, odd = unit(q)
            sent_y[q][0].wait_recv()
            if q in (0, 1, 2, 3):
                hops[q] = send(Y.at[2 + half, odd], Y.at[6, u], XP)
            a = send(Y.at[2 + half, odd], Y.at[2 + half, 2 + odd], CP)
            sent_y[q][1].wait_recv()
            if q not in (0, 1, 2, 3):
                hops[q] = send(Y.at[2 + half, 4 + odd], Y.at[6, u], XM)
            b = send(Y.at[2 + half, 4 + odd], Y.at[2 + half, 6 + odd], CP)
            served[q] = (a, b)

    def pass_y(qs):
        for q in qs:
            hops[q].wait_recv()
            u = zi(q)
            hops_pair[q] = send(Y.at[6, u], Y.at[7, u], CP)

    def take_own(k):
        for part in (0, 1):
            for way, q, peer in ((0, -k, ZP), (1, k, ZM)):
                if k < 4 or part == way:
                    own[k, part, way].wait_recv()
                if k < 3 or (k == 3 and part == way):
                    own[k + 1, part, way] = rows_to(q, y, half_own[part], peer)
        for q in (-k, k) if k < 4 else (4,):
            to_y[q] = rows_to(q, y, wide, YP)

    def take_theirs(k):
        for way, q, peer in ((0, -k, ZP), (1, k, ZM)):
            theirs[k, way].wait_recv()
            if k < 3:
                theirs[k + 1, way] = rows_to(q, other, thin, peer)
            elif k == 3:
                theirs[k + 1, way] = rows_to(q, other, half_thin[way], peer)

    for way, peer in ((0, ZP), (1, ZM)):
        own[1, 1, way] = rows_to(0, y, half_own[1], peer)
    for i in (0, 2, 1, 3):
        pass_hop(i)
    for t in range(3, TICKS):
        early[t].wait_recv()
    for i in range(4):
        hop_pair[i].wait_recv()

    done = []
    for k in range(5):
        qs = [0] if k == 0 else [-k, k] if k < 4 else [4]
        if k < 4:
            take_own(k + 1)
        if k >= 1:
            for q in qs:
                to_y[q].wait_recv()
        products(qs)
        if k >= 1:
            serve(done[-1])
        if k < 4:
            take_theirs(k + 1)
        if k >= 2:
            pass_y(done[-2])
        done.append(qs)

    def add_up(t, m):
        left = G[4 * m : 4 * m + 4, :, :, BLOCK * t : BLOCK * (t + 1)].reshape(256, BLOCK)
        p = dot(left, Y[t].reshape(BLOCK, WIDTH), 0)
        X[4 * m : 4 * m + 4] += quintic_coef * p.reshape(4, UNIT, WIDTH)

    for q in sent_y:
        sent_y[q][2].wait_recv()
    for t in (0, 1):
        for m in range(2):
            add_up(t, m)
    serve([4])
    pass_y([-3, 3])
    for q in served:
        served[q][0].wait_recv()
        served[q][1].wait_recv()
    for t in (2, 3, 4, 5):
        for m in range(2):
            add_up(t, m)
    pass_y([4])
    for m in range(2):
        add_up(6, m)
    for q in hops_pair:
        hops_pair[q].wait_recv()
    stores = []
    for m in range(2):
        add_up(7, m)
        for u in range(4 * m, 4 * m + 4):
            stores.append(pltpu.make_async_copy(X.at[u], o_ref.at[pl.ds(UNIT * u, UNIT)], lsem.at[u]))
            stores[-1].start()
    for copy in started[-SENDS:]:
        copy.wait_send()
    for store in stores:
        store.wait()


def shards(iterate):
    scratch = [
        pltpu.VMEM((8, UNIT, WIDTH), F32),
        pltpu.VMEM((TICKS, 8, UNIT, WIDTH), BF16),
        pltpu.VMEM((TICKS, 8, UNIT, WIDTH), BF16),
        pltpu.VMEM((TICKS, 8, 128, 256), F32),
        pltpu.VMEM((8, 2, 32, ROWS), BF16),
        pltpu.VMEM((TICKS, 2, 128, 256), BF16),
        pltpu.VMEM((TICKS, 2, 128, 256), BF16),
        pltpu.VMEM((TICKS, 2, 128, 128), BF16),
        pltpu.VMEM((TICKS, 2, 128, 128), BF16),
        pltpu.VMEM((TICKS, 2, 128, 256), BF16),
        pltpu.VMEM((TICKS, 2, 128, 256), BF16),
        pltpu.VMEM((TICKS, 2, 128, 256), BF16),
        pltpu.VMEM((TICKS, 2, 64, 256), BF16),
        pltpu.VMEM((TICKS, 2, 64, 256), BF16),
        pltpu.VMEM((6, 8, 32, 256), BF16),
        pltpu.VMEM((6, 8, 32, 256), BF16),
        pltpu.VMEM((TICKS, 64, 256), BF16),
        pltpu.VMEM((TICKS, 64, 256), BF16),
        pltpu.VMEM((2, 32, BLOCK), BF16),
        pltpu.VMEM((8, BLOCK), F32),
        pltpu.VMEM((8, BLOCK), F32),
        pltpu.VMEM((8, 8, BLOCK), F32),
        pltpu.VMEM((2 * UNIT, WIDTH), F32),
        pltpu.SemaphoreType.DMA((MESSAGES,)),
        pltpu.SemaphoreType.DMA((MESSAGES,)),
        pltpu.SemaphoreType.DMA((8,)),
    ]
    return pl.pallas_call(
        kernel,
        out_shape=jax.ShapeDtypeStruct(iterate.shape, F32),
        in_specs=[pl.BlockSpec(memory_space=pl.ANY)],
        out_specs=pl.BlockSpec(memory_space=pl.ANY),
        scratch_shapes=scratch,
        compiler_params=pltpu.CompilerParams(
            collective_id=0, has_side_effects=True, vmem_limit_bytes=60 * 1024 * 1024
        ),
        cost_estimate=pl.CostEstimate(flops=6 * BLOCK * ROWS * WIDTH, bytes_accessed=8 * BLOCK * WIDTH, transcendentals=0),
    )(iterate)


def solution(mesh):
    return jax.shard_map(
        shards,
        mesh=mesh,
        in_specs=(P(("mat", "band"), "col"),),
        out_specs=P(("mat", "band"), "col"),
        check_vma=False,
    )
```
